32 devices in a mesh: expert: 4 (over x, core), context: 2 (over y), dp: 4 (over z).
Axes of the slice: x: 2, y: 2, z: 4, core: 2. Of those that a mesh axis runs over, the one named last changes fastest.
Arguments:
- tokens: bfloat16 [16, 512, 1024], P(('expert', 'dp'), 'context'), may hold values from -6 to 6
- span_order: int32 [4], replicated, may hold values from 0 to 3, each once
- routes: int32 [16, 512, 8], P(('expert', 'dp'), 'context'), may hold values from 0 to 15, all different within a row; in each aligned block of 256 rows (0 to 255, 256 to 511, ..., all dimensions but the last counted through in order) at most 160 rows name the same one
- norm_attn: bfloat16 [1024], replicated, may hold values from 0.5 to 1.5
- w_query: bfloat16 [1024, 1024], replicated, may hold values from -0.1875 to 0.1875
- w_key: bfloat16 [1024, 512], replicated, may hold values from -0.1875 to 0.1875
- w_value: bfloat16 [1024, 512], replicated, may hold values from -0.1875 to 0.1875
- w_out: bfloat16 [1024, 1024], replicated, may hold values from -1.5 to 1.5
- norm_moe: bfloat16 [1024], replicated, may hold values from 0.5 to 1.5
- w_router: bfloat16 [1024, 16], replicated, may hold values from -0.09375 to 0.09375
- w_gate: bfloat16 [16, 1024, 512], P('expert'), may hold values from -0.1875 to 0.1875
- w_up: bfloat16 [16, 1024, 512], P('expert'), may hold values from -0.1875 to 0.1875
- w_down: bfloat16 [16, 512, 1024], P('expert'), may hold values from -1 to 1
- cotangent: bfloat16 [16, 512, 1024], P(('expert', 'dp'), 'context'), may hold values from -6 to 6
Outputs:
- outputs: bfloat16 [16, 512, 1024], P(('expert', 'dp'), 'context')
- grad_tokens: bfloat16 [16, 512, 1024], P(('expert', 'dp'), 'context')
- grad_norm_attn: float32 [1024], replicated
- grad_query: float32 [1024, 1024], replicated
- grad_key: float32 [1024, 512], replicated
- grad_value: float32 [1024, 512], replicated
- grad_out: float32 [1024, 1024], replicated
- grad_norm_moe: float32 [1024], replicated
- grad_router: float32 [1024, 16], replicated
- grad_gate: float32 [16, 1024, 512], P('expert')
- grad_up: float32 [16, 1024, 512], P('expert')
- grad_down: float32 [16, 512, 1024], P('expert')
The draws below stay inside these ranges and needn't reach their ends.
Inputs may be any that keep to these rules, and one draw needn't show every extreme that they name: span_order is a permutation; stored block j of every sequence holds the tokens at positions span_order[j] * 128 to span_order[j] * 128 + 127. `routes`: each token names 8 different experts. Within the rows of one device (aligned blocks of 256 rows, in order), no expert is named by more than 160 rows, a bound that some block reaches.
All inputs are finite; a program needn't handle non-finite values.
Results may differ from the reference program's by a relative error of at most 0.017.
Values may be sent and summed in bfloat16 or wider, within the bound.
A program may use at most 192 MiB of HBM per device.

```python
import math
import jax
import jax.numpy as jnp
import numpy as np
from jax import lax

D = 1024
H = 16
KV = 8
HD = 64
FF = 512
TOP = 8
EXPERTS = 16
TOK_DEV = 256
CAP = 160
SPAN = 128
SPANS = 4
SEQ_LEN = 512
SEQS = 16


def block_scale(key, shape, pieces, smallest, high):
    level = 1.0
    for position, parts in pieces:
        steps = jax.random.uniform(jax.random.fold_in(jax.random.fold_in(key, 6), position), (parts,), jnp.float32, smallest / len(pieces), high / len(pieces))
        level = level * jnp.repeat(jnp.exp(steps), shape[position] // parts).reshape((-1,) + (1,) * (len(shape) - 1 - position))
    return level


def deal_out(own_key, own, number, rows, number_of, top, limit, lean):
    ranking = jax.random.permutation(own_key, number_of)
    crowded, common = shares(number_of, rows * top, limit, lean, True), shares(number_of, rows * top, limit, lean, False)
    places = jnp.arange(number_of)

    def named(lengths, offset_by):
        used = int((lengths > 0).sum())
        fixed = max(1, used // 4)
        moved = fixed + (places - fixed + offset_by * (used - fixed)) % max(1, number_of - fixed)
        return jnp.zeros((number_of,), jnp.int32).at[ranking[jnp.where(places < fixed, places, moved)]].set(jnp.asarray(lengths, jnp.int32))

    lengths = jnp.where(number % 4 == 0, named(crowded, number // 4), named(common, number - number // 4 - 1))
    mixed = jax.random.permutation(jax.random.fold_in(own, 3), number_of)
    giver, taker = mixed[0:number_of // 2 * 2:2], mixed[1:number_of // 2 * 2:2]
    margin = jnp.minimum(lengths[giver] - 1, limit - lengths[taker]) // 2
    margin = jnp.where((giver == ranking[0]) | (taker == ranking[0]) | (lengths[taker] == 0), 0, jnp.maximum(margin, 0))
    moved = jax.random.randint(jax.random.fold_in(own, 4), (number_of // 2,), 0, 1 << 20) % (margin + 1)
    lengths = lengths.at[giver].add(-moved).at[taker].add(moved)
    labels = jnp.searchsorted(jnp.cumsum(lengths), jnp.arange(rows * top), side="right").astype(jnp.int32)
    listing = labels.reshape(top, rows).T
    listing = listing[jax.random.permutation(jax.random.fold_in(own, 1), rows)]
    offset_by = jax.random.randint(jax.random.fold_in(own, 2), (rows, 1), 0, top)
    return jnp.take_along_axis(listing, (jnp.arange(top)[None, :] + offset_by) % top, axis=1)


def shares(number_of, total, reach, lean, full):
    loads = [(1 << 20) // math.isqrt(standing ** lean) + 1 for standing in range(1, number_of + 1)]
    largest = reach if full else min(reach, max(-(-total // number_of), total * loads[0] // sum(loads)))
    least = 1 if total - largest >= number_of - 1 else 0
    given, spare = [largest] + [least] * (number_of - 1), total - largest - least * (number_of - 1)
    while spare > 0:
        free = [i for i in range(1, number_of) if given[i] < largest] or [i for i in range(1, number_of) if given[i] < reach]
        mass, budget = sum([loads[i] for i in free]), spare
        for i in free:
            addition = min(reach - given[i], max(1, budget * loads[i] // mass), spare)
            given[i] = given[i] + addition
            spare = spare - addition
    return np.array(given)


def gaussian(own_key, shape, width, limit, split=(), kind=jnp.bfloat16):
    values = jax.random.normal(own_key, shape, jnp.float32) * width
    if len(split) > 0:
        values = block_scale(own_key, shape, split, -0.22, 0.18) * values
    return jnp.clip(values, min=-limit, max=limit).astype(kind)


def setup_inputs(seed: int = 0) -> dict:
    keys = jax.random.split(jax.random.key(seed), 15)
    tokens = gaussian(keys[0], (SEQS, SEQ_LEN, D), 1.0, 6.0, ((0, 16), (1, 2)))
    span_order = jax.random.permutation(keys[1], SPANS).astype(jnp.int32)
    routes_keys = jax.random.split(jax.random.fold_in(keys[2], 1), SEQS * SEQ_LEN // TOK_DEV)
    routes_turns = jax.random.permutation(jax.random.fold_in(keys[2], 3), SEQS * SEQ_LEN // TOK_DEV)
    routes = jax.vmap(lambda own, number: deal_out(jax.random.fold_in(keys[2], 2), own, number, TOK_DEV, EXPERTS, TOP, CAP, 1))(routes_keys, routes_turns).reshape((SEQS, SEQ_LEN, TOP))
    norm_attn = jnp.clip(1.0 + 0.1 * jax.random.normal(keys[3], (D,), jnp.float32), 0.5, 1.5).astype(jnp.bfloat16)
    w_query = gaussian(keys[4], (D, H * HD), D ** -0.5, 0.1875)
    w_key = gaussian(keys[5], (D, KV * HD), D ** -0.5, 0.1875)
    w_value = gaussian(keys[6], (D, KV * HD), D ** -0.5, 0.1875)
    w_out = gaussian(keys[7], (H * HD, D), (H * HD // 64) ** -0.5, 1.5)
    norm_moe = jnp.clip(1.0 + 0.1 * jax.random.normal(keys[8], (D,), jnp.float32), 0.5, 1.5).astype(jnp.bfloat16)
    w_router = gaussian(keys[9], (D, EXPERTS), (4 * D) ** -0.5, 0.09375)
    w_gate = gaussian(keys[10], (EXPERTS, D, FF), D ** -0.5, 0.1875, ((0, 4),))
    w_up = gaussian(keys[11], (EXPERTS, D, FF), D ** -0.5, 0.1875, ((0, 4),))
    w_down = gaussian(keys[12], (EXPERTS, FF, D), (FF // 16) ** -0.5, 1.0, ((0, 4),))
    cotangent = gaussian(keys[13], (SEQS, SEQ_LEN, D), 1.0, 6.0, ((0, 16), (1, 2)))
    return dict(tokens=tokens, span_order=span_order, routes=routes, norm_attn=norm_attn, w_query=w_query, w_key=w_key, w_value=w_value, w_out=w_out, norm_moe=norm_moe, w_router=w_router, w_gate=w_gate, w_up=w_up, w_down=w_down, cotangent=cotangent)


EPSILON = 1e-06
ROPE_BASE = 10000.0
MASKED = -1e+30

@jax.custom_vjp
def low(v):
    return lax.optimization_barrier(v.astype(jnp.bfloat16)).astype(jnp.float32)

@jax.custom_vjp
def low_back(v):
    return v

def low_keep(v):
    return (low(v), None)

def low_pass(kept, grad):
    return (grad,)

def back_keep(v):
    return (v, None)

def back_low(kept, grad):
    return (low(grad),)
low.defvjp(low_keep, low_pass)
low_back.defvjp(back_keep, back_low)

def highest(left_mat, right_mat):
    return jnp.dot(left_mat, right_mat, precision=lax.Precision.HIGHEST)

def rms_scale(values, norm_gain):
    return values * lax.rsqrt(lax.optimization_barrier(jnp.mean(values * values, axis=-1, keepdims=True)) + EPSILON) * norm_gain

def rope_tables(positions):
    half_dim = HD // 2
    frequency = ROPE_BASE ** (-(jnp.arange(half_dim, dtype=jnp.float32) * 2.0) / HD)
    angles = positions.astype(jnp.float32)[:, None] * frequency[None, :]
    return (jnp.cos(angles), jnp.sin(angles))

def rotate(tensor, cos_table, sin_table):
    half_dim = tensor.shape[-1] // 2
    front_half = tensor[..., :half_dim]
    back_half = tensor[..., half_dim:]
    cos_wide = cos_table[:, None, :]
    sin_wide = sin_table[:, None, :]
    return jnp.concatenate([front_half * cos_wide - back_half * sin_wide, back_half * cos_wide + front_half * sin_wide], axis=-1)

def slot_tables(route_rows):
    flat_ids = route_rows.reshape(-1)
    assignments = flat_ids.shape[0]
    one_hot = (flat_ids[:, None] == jnp.arange(EXPERTS, dtype=jnp.int32)[None, :]).astype(jnp.int32)
    earlier = jnp.cumsum(one_hot, axis=0, dtype=jnp.int32) - one_hot
    within = lax.optimization_barrier(jnp.sum(earlier * one_hot, axis=1, dtype=jnp.int32))
    target = flat_ids * CAP + within
    source = jnp.full((EXPERTS * CAP,), assignments, jnp.int32).at[target].set(jnp.arange(assignments, dtype=jnp.int32))
    filled = source < assignments
    return (target, jnp.minimum(source, assignments - 1), filled)

def take_rows(table_rows, row_ids):
    return jnp.take(table_rows, row_ids, axis=0)

def layer(inputs, route_rows, cos_table, sin_table, allowed, params):
    norm_attn, w_query, w_key, w_value, w_out, norm_moe, w_router, w_gate, w_up, w_down = params
    seq_len = inputs.shape[0]
    groups = H // KV
    score_scale = 1.0 / math.sqrt(HD)
    h_one = low(rms_scale(inputs, norm_attn))
    queries = low(rotate(low_back(highest(h_one, w_query)).reshape(seq_len, H, HD), cos_table, sin_table))
    key_heads = low(rotate(low_back(highest(h_one, w_key)).reshape(seq_len, KV, HD), cos_table, sin_table))
    value_heads = low(low_back(highest(h_one, w_value))).reshape(seq_len, KV, HD)
    scores = jnp.einsum('qkgd,skd->kgqs', queries.reshape(seq_len, KV, groups, HD), key_heads, precision=lax.Precision.HIGHEST) * score_scale
    scores = low_back(scores)
    masked = jnp.where(allowed, scores, MASKED)
    exp_scores = jnp.exp(masked - lax.optimization_barrier(jnp.max(masked, axis=-1, keepdims=True)))
    attn_probs = exp_scores / lax.optimization_barrier(jnp.sum(exp_scores, axis=-1, keepdims=True))
    mixed_heads = jnp.einsum('kgqs,skd->qkgd', low(attn_probs), value_heads, precision=lax.Precision.HIGHEST).reshape(seq_len, H * HD)
    mixed_heads = low(low_back(mixed_heads))
    y_one = inputs + low_back(highest(mixed_heads, w_out))
    h_two = low(rms_scale(y_one, norm_moe))
    logits = low_back(highest(h_two, w_router))
    chosen_mask = route_rows[:, :, None] == jnp.arange(EXPERTS, dtype=jnp.int32)[None, None, :]
    chosen = lax.optimization_barrier(jnp.sum(jnp.where(chosen_mask, logits[:, None, :], 0.0), axis=-1))
    chosen_exp = jnp.exp(chosen - lax.optimization_barrier(jnp.max(chosen, axis=-1, keepdims=True)))
    route_weights = chosen_exp / lax.optimization_barrier(jnp.sum(chosen_exp, axis=-1, keepdims=True))
    blocks = seq_len // TOK_DEV
    block_h = h_two.reshape(blocks, TOK_DEV, D)
    target, source, filled = jax.vmap(slot_tables)(route_rows.reshape(blocks, TOK_DEV, TOP))
    taken_rows = jax.vmap(take_rows)(block_h, source // TOP)
    sent_rows = low_back(jnp.where(filled[:, :, None], taken_rows, 0.0)).reshape(blocks, EXPERTS, CAP, D)
    gate_pre = low_back(jnp.einsum('becd,edf->becf', sent_rows, w_gate, precision=lax.Precision.HIGHEST))
    upward = low_back(jnp.einsum('becd,edf->becf', sent_rows, w_up, precision=lax.Precision.HIGHEST))
    hidden = low(jax.nn.silu(gate_pre) * upward)
    produced = low(low_back(jnp.einsum('becf,efd->becd', hidden, w_down, precision=lax.Precision.HIGHEST)))
    produced = produced.reshape(blocks, EXPERTS * CAP, D)
    gathered = jax.vmap(take_rows)(produced, target).reshape(seq_len, TOP, D)
    y_two = lax.optimization_barrier(jnp.sum(route_weights[:, :, None] * gathered, axis=1))
    return y_one + y_two

def reference(tokens, span_order, routes, norm_attn, w_query, w_key, w_value, w_out, norm_moe, w_router, w_gate, w_up, w_down, cotangent):
    params = tuple((weight_arg.astype(jnp.float32) for weight_arg in (norm_attn, w_query, w_key, w_value, w_out, norm_moe, w_router, w_gate, w_up, w_down)))
    row_index = jnp.arange(SEQ_LEN, dtype=jnp.int32)
    positions = (span_order[row_index // SPAN] * SPAN + row_index % SPAN).astype(jnp.int32)
    cos_table, sin_table = rope_tables(positions)
    allowed = positions[None, :] <= positions[:, None]

    def one_sequence(running, seq_item):
        seq_tokens, seq_routes, seq_cot = seq_item

        def forward(inputs, weights):
            return layer(inputs, seq_routes, cos_table, sin_table, allowed, weights)
        result, pull = jax.vjp(forward, seq_tokens.astype(jnp.float32), params)
        grad_inputs, grad_params = pull(seq_cot.astype(jnp.float32))
        running = tuple((prior + latest for prior, latest in zip(running, grad_params)))
        return (running, (result.astype(jnp.bfloat16), grad_inputs.astype(jnp.bfloat16)))
    zero_grads = tuple((jnp.zeros_like(weight_arg) for weight_arg in params))
    totals, (outputs, grad_tokens) = lax.scan(one_sequence, zero_grads, (tokens, routes, cotangent))
    return (outputs, grad_tokens, totals[0], totals[1], totals[2], totals[3], totals[4], totals[5], totals[6], totals[7], totals[8], totals[9])
```

```python
import math

import jax
import jax.numpy as jnp
from jax import lax
from jax.sharding import PartitionSpec as P

H = 16
KV = 8
HD = 64
EXPERTS = 16
SPAN = 128

EPSILON = 1e-06
ROPE_BASE = 10000.0
MASKED = -1e30
F32 = jnp.float32
BF16 = jnp.bfloat16


def rope_tables(positions):
    half_dim = HD // 2
    frequency = ROPE_BASE ** (-(jnp.arange(half_dim, dtype=F32) * 2.0) / HD)
    angles = positions.astype(F32)[:, None] * frequency[None, :]
    return (jnp.cos(angles), jnp.sin(angles))


def rotate(tensor, cos_table, sin_table):
    half_dim = tensor.shape[-1] // 2
    front = tensor[..., :half_dim]
    back = tensor[..., half_dim:]
    cos_wide = cos_table[:, None, :]
    sin_wide = sin_table[:, None, :]
    return jnp.concatenate(
        [front * cos_wide - back * sin_wide, back * cos_wide + front * sin_wide], axis=-1
    )


def positions_of(row_index, span_order):
    block_ids = row_index // SPAN
    picked = jnp.where(
        block_ids[:, None] == jnp.arange(span_order.shape[0], dtype=jnp.int32)[None, :],
        span_order[None, :],
        0,
    )
    return jnp.sum(picked, axis=1, dtype=jnp.int32) * SPAN + row_index % SPAN


def norm_back(grad_normed, normed, inv_root):
    return inv_root * (
        grad_normed - normed * jnp.mean(grad_normed * normed, axis=-1, keepdims=True)
    )


def dot(a, b):
    return jnp.dot(a, b, preferred_element_type=F32)


def dot_t(a, b):
    return lax.dot_general(a, b, (((1,), (1,)), ((), ())), preferred_element_type=F32)


def t_dot(a, b):
    return lax.dot_general(a, b, (((0,), (0,)), ((), ())), preferred_element_type=F32)


def body(
    tokens,
    span_order,
    routes,
    norm_attn,
    w_query,
    w_key,
    w_value,
    w_out,
    norm_moe,
    w_router,
    w_gate,
    w_up,
    w_down,
    cotangent,
):
    tok_rows = tokens.shape[1]
    width = tokens.shape[2]
    seq_rows = tok_rows * lax.axis_size("context")
    groups = H // KV
    score_scale = 1.0 / math.sqrt(HD)
    local_experts = w_gate.shape[0]
    ff = w_gate.shape[2]
    dy_all = lax.all_gather(cotangent[0], "expert", axis=0, tiled=True)
    routes_all = lax.all_gather(routes[0], "expert", axis=0, tiled=True)

    local_index = lax.axis_index("context") * tok_rows + jnp.arange(tok_rows, dtype=jnp.int32)
    pos_query = positions_of(local_index, span_order)
    pos_keys = positions_of(jnp.arange(seq_rows, dtype=jnp.int32), span_order)
    cos_table, sin_table = rope_tables(pos_query)
    allowed = pos_keys[None, :] <= pos_query[:, None]
    inputs = tokens[0].astype(F32)
    inv_one = lax.rsqrt(jnp.mean(inputs * inputs, axis=-1, keepdims=True) + EPSILON)
    normed_one = inputs * inv_one
    gain_one = norm_attn.astype(F32)
    h_one = (normed_one * gain_one).astype(BF16)
    key_pre = dot(h_one, w_key).reshape(tok_rows, KV, HD)
    keys_local = rotate(key_pre, cos_table, sin_table).astype(BF16).reshape(tok_rows, KV * HD)
    values_local = dot(h_one, w_value).astype(BF16)
    kv_all = lax.all_gather(
        jnp.concatenate([keys_local, values_local], axis=1), "context", axis=0, tiled=True
    )
    query_pre = dot(h_one, w_query).reshape(tok_rows, H, HD)
    queries = (
        rotate(query_pre, cos_table, sin_table).astype(BF16).reshape(tok_rows, KV, groups, HD)
    )
    keys_all = kv_all[:, : KV * HD].reshape(seq_rows, KV, HD)
    values_all = kv_all[:, KV * HD :].reshape(seq_rows, KV, HD)
    scores = (
        jnp.einsum("qkgd,skd->kgqs", queries, keys_all, preferred_element_type=F32) * score_scale
    )
    masked = jnp.where(allowed, scores, MASKED)
    top_score = jnp.max(masked, axis=-1, keepdims=True)
    exp_scores = jnp.exp(masked - top_score)
    total_exp = jnp.sum(exp_scores, axis=-1, keepdims=True)
    attn_probs = exp_scores / total_exp
    probs_rounded = attn_probs.astype(BF16)
    mixed_heads = jnp.einsum(
        "kgqs,skd->qkgd", probs_rounded, values_all, preferred_element_type=F32
    )
    mixed_heads = mixed_heads.reshape(tok_rows, H * HD).astype(BF16)
    y_one = inputs + dot(mixed_heads, w_out)
    inv_two = lax.rsqrt(jnp.mean(y_one * y_one, axis=-1, keepdims=True) + EPSILON)
    normed_two = y_one * inv_two
    gain_two = norm_moe.astype(F32)
    h_two = (normed_two * gain_two).astype(BF16)
    h_all = lax.all_gather(h_two, "expert", axis=0, tiled=True)

    experts = jnp.arange(EXPERTS, dtype=jnp.int32)
    chosen = jnp.any(routes_all[:, :, None] == experts[None, None, :], axis=1)
    logits = jnp.where(chosen, dot(h_all, w_router), MASKED)
    weights = jnp.where(chosen, jnp.exp(logits - jnp.max(logits, axis=-1, keepdims=True)), 0.0)
    weights = weights / jnp.sum(weights, axis=-1, keepdims=True)
    me = lax.axis_index("expert")
    mine = lax.dynamic_slice_in_dim(weights, me * local_experts, local_experts, axis=1)

    partial_y = None
    partial_h = None
    dots = []
    g_gate, g_up, g_down = [], [], []
    for e in range(local_experts):
        weight = mine[:, e : e + 1]
        gate_pre = dot(h_all, w_gate[e])
        upward = dot(h_all, w_up[e])
        back = dot_t(dy_all, w_down[e])
        sigmoid_gate = jax.nn.sigmoid(gate_pre)
        silu_gate = gate_pre * sigmoid_gate
        hidden = silu_gate * upward
        hidden_w = (hidden * weight).astype(BF16)
        dots.append(jnp.sum(hidden * back, axis=-1, keepdims=True))
        grad_hidden = back * weight
        grad_gate_pre = (
            grad_hidden * upward * sigmoid_gate * (1.0 + gate_pre * (1.0 - sigmoid_gate))
        ).astype(BF16)
        grad_up_pre = (grad_hidden * silu_gate).astype(BF16)
        add_y = dot(hidden_w, w_down[e])
        add_h = dot_t(grad_gate_pre, w_gate[e]) + dot_t(grad_up_pre, w_up[e])
        partial_y = add_y if partial_y is None else partial_y + add_y
        partial_h = add_h if partial_h is None else partial_h + add_h
        g_down.append(t_dot(hidden_w, dy_all).astype(BF16))
        g_gate.append(t_dot(h_all, grad_gate_pre).astype(BF16))
        g_up.append(t_dot(h_all, grad_up_pre).astype(BF16))

    d_weights = jnp.concatenate(dots, axis=1)
    d_wide = lax.dynamic_update_slice_in_dim(
        jnp.zeros((d_weights.shape[0], EXPERTS), F32), d_weights, me * local_experts, axis=1
    )
    d_high = lax.reduce_precision(d_wide, 8, 7)
    packed = jnp.concatenate(
        [
            partial_h.astype(BF16),
            d_high.astype(BF16),
            (d_wide - d_high).astype(BF16),
            jnp.zeros((d_wide.shape[0], 128 - 2 * EXPERTS), BF16),
        ],
        axis=1,
    )
    home = lax.psum_scatter(packed, "expert", scatter_dimension=0, tiled=True).astype(F32)
    y_two = lax.psum_scatter(
        partial_y.astype(BF16), "expert", scatter_dimension=0, tiled=True
    ).astype(F32)
    total_gate, total_up, total_down = (
        lax.psum(jnp.stack(g), ("context", "dp")).astype(F32) for g in (g_gate, g_up, g_down)
    )
    outputs = (y_one + y_two).astype(BF16)[None]

    grad_final = cotangent[0].astype(F32)
    grad_weights = home[:, width : width + EXPERTS] + home[:, width + EXPERTS : width + 2 * EXPERTS]
    own = lax.dynamic_slice_in_dim(weights, me * tok_rows, tok_rows, axis=0)
    grad_logits = (
        own * (grad_weights - jnp.sum(own * grad_weights, axis=-1, keepdims=True))
    ).astype(BF16)
    grad_router_w = t_dot(h_two, grad_logits)
    grad_h_two = home[:, :width] + dot_t(grad_logits, w_router)
    grad_gain_two = jnp.sum(grad_h_two * normed_two, axis=0)
    grad_y_one = grad_final + norm_back(grad_h_two * gain_two, normed_two, inv_two)
    grad_attn = grad_y_one.astype(BF16)
    grad_out_w = t_dot(mixed_heads, grad_attn)
    grad_mixed = dot_t(grad_attn, w_out).astype(BF16).reshape(tok_rows, KV, groups, HD)
    grad_probs = jnp.einsum("qkgd,skd->kgqs", grad_mixed, values_all, preferred_element_type=F32)
    grad_values = jnp.einsum(
        "kgqs,qkgd->skd", probs_rounded, grad_mixed, preferred_element_type=F32
    )
    row_dots = jnp.sum(attn_probs * grad_probs, axis=-1, keepdims=True)
    grad_scores = (attn_probs * (grad_probs - row_dots)).astype(BF16)
    grad_keys = (
        jnp.einsum("kgqs,qkgd->skd", grad_scores, queries, preferred_element_type=F32)
        * score_scale
    )
    grad_kv = lax.psum_scatter(
        jnp.concatenate(
            [grad_keys.reshape(seq_rows, KV * HD), grad_values.reshape(seq_rows, KV * HD)], axis=1
        ).astype(BF16),
        "context",
        scatter_dimension=0,
        tiled=True,
    ).astype(F32)
    grad_queries = (
        jnp.einsum("kgqs,skd->qkgd", grad_scores, keys_all, preferred_element_type=F32)
        * score_scale
    )
    grad_q_pre = (
        rotate(grad_queries.reshape(tok_rows, H, HD), cos_table, -sin_table)
        .reshape(tok_rows, H * HD)
        .astype(BF16)
    )
    grad_k_pre = (
        rotate(grad_kv[:, : KV * HD].reshape(tok_rows, KV, HD), cos_table, -sin_table)
        .reshape(tok_rows, KV * HD)
        .astype(BF16)
    )
    grad_v_pre = grad_kv[:, KV * HD :].astype(BF16)
    grad_query_w = t_dot(h_one, grad_q_pre)
    grad_key_w = t_dot(h_one, grad_k_pre)
    grad_value_w = t_dot(h_one, grad_v_pre)
    grad_h_one = (
        dot_t(grad_q_pre, w_query) + dot_t(grad_k_pre, w_key) + dot_t(grad_v_pre, w_value)
    )
    grad_gain_one = jnp.sum(grad_h_one * normed_one, axis=0)
    grad_inputs = grad_y_one + norm_back(grad_h_one * gain_one, normed_one, inv_one)
    grad_tokens = grad_inputs.astype(BF16)[None]
    everywhere = ("expert", "context", "dp")
    total_o = lax.psum(grad_out_w.astype(BF16), everywhere).astype(F32)
    total_q, total_k, total_v = (
        t.astype(F32)
        for t in lax.psum(
            tuple(g.astype(BF16) for g in (grad_query_w, grad_key_w, grad_value_w)), everywhere
        )
    )
    total_g1, total_g2, total_r = lax.psum(
        (grad_gain_one, grad_gain_two, grad_router_w), everywhere
    )
    return (
        outputs,
        grad_tokens,
        total_g1,
        total_q,
        total_k,
        total_v,
        total_o,
        total_g2,
        total_r,
        total_gate,
        total_up,
        total_down,
    )


def solution(mesh):
    in_specs = (
        P(("expert", "dp"), "context", None),
        P(),
        P(("expert", "dp"), "context", None),
        P(),
        P(),
        P(),
        P(),
        P(),
        P(),
        P(),
        P("expert", None, None),
        P("expert", None, None),
        P("expert", None, None),
        P(("expert", "dp"), "context", None),
    )
    out_specs = (
        P(("expert", "dp"), "context", None),
        P(("expert", "dp"), "context", None),
        P(),
        P(),
        P(),
        P(),
        P(),
        P(),
        P(),
        P("expert", None, None),
        P("expert", None, None),
        P("expert", None, None),
    )
    return jax.shard_map(body, mesh=mesh, in_specs=in_specs, out_specs=out_specs, check_vma=False)
```

```python
import math

import jax
import jax.numpy as jnp
from jax import lax
from jax.sharding import PartitionSpec as P

H = 16
KV = 8
HD = 64
EXPERTS = 16
SPAN = 128

EPSILON = 1e-06
ROPE_BASE = 10000.0
MASKED = -1e30
F32 = jnp.float32
BF16 = jnp.bfloat16


def rope_tables(positions):
    half_dim = HD // 2
    frequency = ROPE_BASE ** (-(jnp.arange(half_dim, dtype=F32) * 2.0) / HD)
    angles = positions.astype(F32)[:, None] * frequency[None, :]
    return (jnp.cos(angles), jnp.sin(angles))


def rotate(tensor, cos_table, sin_table):
    half_dim = tensor.shape[-1] // 2
    front = tensor[..., :half_dim]
    back = tensor[..., half_dim:]
    cos_wide = cos_table[:, None, :]
    sin_wide = sin_table[:, None, :]
    return jnp.concatenate(
        [front * cos_wide - back * sin_wide, back * cos_wide + front * sin_wide], axis=-1
    )


def positions_of(row_index, span_order):
    block_ids = row_index // SPAN
    picked = jnp.where(
        block_ids[:, None] == jnp.arange(span_order.shape[0], dtype=jnp.int32)[None, :],
        span_order[None, :],
        0,
    )
    return jnp.sum(picked, axis=1, dtype=jnp.int32) * SPAN + row_index % SPAN


def norm_back(grad_normed, normed, inv_root):
    return inv_root * (
        grad_normed - normed * jnp.mean(grad_normed * normed, axis=-1, keepdims=True)
    )


def dot(a, b):
    return jnp.dot(a, b, preferred_element_type=F32)


def dot_t(a, b):
    return lax.dot_general(a, b, (((1,), (1,)), ((), ())), preferred_element_type=F32)


def t_dot(a, b):
    return lax.dot_general(a, b, (((0,), (0,)), ((), ())), preferred_element_type=F32)


def ring_sum(gate, up, down):
    axes = ("context", "dp")
    inner = lax.axis_size("dp")
    size = lax.axis_size("context") * inner
    place = [
        c * inner + (d if c % 2 == 0 else inner - 1 - d)
        for c in range(size // inner)
        for d in range(inner)
    ]
    order = sorted(range(size), key=lambda i: place[i])
    pos = jnp.array(place, jnp.int32)[lax.axis_index(axes)]
    shapes = [a.shape for a in (gate, up, down)]
    gate, up, down = (a.reshape(2, size, -1, a.shape[-1]) for a in (gate, up, down))
    rows, half = gate.shape[2], gate.shape[3]

    def piece(way, index):
        g, u, d = (
            lax.dynamic_index_in_dim(a[way], index, 0, keepdims=False) for a in (gate, up, down)
        )
        return jnp.concatenate([jnp.concatenate([g, u], axis=1), d], axis=0)

    step_of = (1, -1)
    perms = [[(order[i], order[(i + t) % size]) for i in range(size)] for t in step_of]
    held = [piece(way, pos) for way in range(2)]
    for s in range(size - 1):
        for way, t in enumerate(step_of):
            came = lax.ppermute(held[way], axes, perms[way])
            own = piece(way, lax.rem(pos - t * (s + 1) + size, size))
            held[way] = (came.astype(F32) + own.astype(F32)).astype(BF16)
    totals = [jnp.zeros(a.shape, F32) for a in (gate, up, down)]
    for s in range(size):
        for way, t in enumerate(step_of):
            index = lax.rem(pos + t * (1 - s) + size, size)
            now = held[way]
            if s < size - 1:
                held[way] = lax.ppermute(now, axes, perms[way])
            for i, part in enumerate((now[:rows, :half], now[:rows, half:], now[rows:])):
                totals[i] = lax.dynamic_update_slice(
                    totals[i], part.astype(F32)[None, None], (way, index, 0, 0)
                )
    return [a.reshape(shape) for a, shape in zip(totals, shapes)]


def body(
    tokens,
    span_order,
    routes,
    norm_attn,
    w_query,
    w_key,
    w_value,
    w_out,
    norm_moe,
    w_router,
    w_gate,
    w_up,
    w_down,
    cotangent,
):
    tok_rows = tokens.shape[1]
    width = tokens.shape[2]
    seq_rows = tok_rows * lax.axis_size("context")
    groups = H // KV
    score_scale = 1.0 / math.sqrt(HD)
    local_experts = w_gate.shape[0]
    ff = w_gate.shape[2]
    dy_all = lax.all_gather(cotangent[0], "expert", axis=0, tiled=True)
    routes_all = lax.all_gather(routes[0], "expert", axis=0, tiled=True)

    local_index = lax.axis_index("context") * tok_rows + jnp.arange(tok_rows, dtype=jnp.int32)
    pos_query = positions_of(local_index, span_order)
    pos_keys = positions_of(jnp.arange(seq_rows, dtype=jnp.int32), span_order)
    cos_table, sin_table = rope_tables(pos_query)
    allowed = pos_keys[None, :] <= pos_query[:, None]
    inputs = tokens[0].astype(F32)
    inv_one = lax.rsqrt(jnp.mean(inputs * inputs, axis=-1, keepdims=True) + EPSILON)
    normed_one = inputs * inv_one
    gain_one = norm_attn.astype(F32)
    h_one = (normed_one * gain_one).astype(BF16)
    key_pre = dot(h_one, w_key).reshape(tok_rows, KV, HD)
    keys_local = rotate(key_pre, cos_table, sin_table).astype(BF16).reshape(tok_rows, KV * HD)
    values_local = dot(h_one, w_value).astype(BF16)
    kv_all = lax.all_gather(
        jnp.concatenate([keys_local, values_local], axis=1), "context", axis=0, tiled=True
    )
    query_pre = dot(h_one, w_query).reshape(tok_rows, H, HD)
    queries = (
        rotate(query_pre, cos_table, sin_table).astype(BF16).reshape(tok_rows, KV, groups, HD)
    )
    keys_all = kv_all[:, : KV * HD].reshape(seq_rows, KV, HD)
    values_all = kv_all[:, KV * HD :].reshape(seq_rows, KV, HD)
    scores = (
        jnp.einsum("qkgd,skd->kgqs", queries, keys_all, preferred_element_type=F32) * score_scale
    )
    masked = jnp.where(allowed, scores, MASKED)
    top_score = jnp.max(masked, axis=-1, keepdims=True)
    exp_scores = jnp.exp(masked - top_score)
    total_exp = jnp.sum(exp_scores, axis=-1, keepdims=True)
    attn_probs = exp_scores / total_exp
    probs_rounded = attn_probs.astype(BF16)
    mixed_heads = jnp.einsum(
        "kgqs,skd->qkgd", probs_rounded, values_all, preferred_element_type=F32
    )
    mixed_heads = mixed_heads.reshape(tok_rows, H * HD).astype(BF16)
    y_one = inputs + dot(mixed_heads, w_out)
    inv_two = lax.rsqrt(jnp.mean(y_one * y_one, axis=-1, keepdims=True) + EPSILON)
    normed_two = y_one * inv_two
    gain_two = norm_moe.astype(F32)
    h_two = (normed_two * gain_two).astype(BF16)
    h_all = lax.all_gather(h_two, "expert", axis=0, tiled=True)

    experts = jnp.arange(EXPERTS, dtype=jnp.int32)
    chosen = jnp.any(routes_all[:, :, None] == experts[None, None, :], axis=1)
    logits = jnp.where(chosen, dot(h_all, w_router), MASKED)
    weights = jnp.where(chosen, jnp.exp(logits - jnp.max(logits, axis=-1, keepdims=True)), 0.0)
    weights = weights / jnp.sum(weights, axis=-1, keepdims=True)
    me = lax.axis_index("expert")
    mine = lax.dynamic_slice_in_dim(weights, me * local_experts, local_experts, axis=1)

    partial_y = None
    partial_h = None
    dots = []
    g_gate, g_up, g_down = [], [], []
    for e in range(local_experts):
        weight = mine[:, e : e + 1]
        gate_pre = dot(h_all, w_gate[e])
        upward = dot(h_all, w_up[e])
        back = dot_t(dy_all, w_down[e])
        sigmoid_gate = jax.nn.sigmoid(gate_pre)
        silu_gate = gate_pre * sigmoid_gate
        hidden = silu_gate * upward
        hidden_w = (hidden * weight).astype(BF16)
        dots.append(jnp.sum(hidden * back, axis=-1, keepdims=True))
        grad_hidden = back * weight
        grad_gate_pre = (
            grad_hidden * upward * sigmoid_gate * (1.0 + gate_pre * (1.0 - sigmoid_gate))
        ).astype(BF16)
        grad_up_pre = (grad_hidden * silu_gate).astype(BF16)
        add_y = dot(hidden_w, w_down[e])
        add_h = dot_t(grad_gate_pre, w_gate[e]) + dot_t(grad_up_pre, w_up[e])
        partial_y = add_y if partial_y is None else partial_y + add_y
        partial_h = add_h if partial_h is None else partial_h + add_h
        g_down.append(t_dot(hidden_w, dy_all).astype(BF16))
        g_gate.append(t_dot(h_all, grad_gate_pre).astype(BF16))
        g_up.append(t_dot(h_all, grad_up_pre).astype(BF16))

    d_weights = jnp.concatenate(dots, axis=1)
    d_wide = lax.dynamic_update_slice_in_dim(
        jnp.zeros((d_weights.shape[0], EXPERTS), F32), d_weights, me * local_experts, axis=1
    )
    d_high = lax.reduce_precision(d_wide, 8, 7)
    packed = jnp.concatenate(
        [
            partial_h.astype(BF16),
            d_high.astype(BF16),
            (d_wide - d_high).astype(BF16),
            jnp.zeros((d_wide.shape[0], 128 - 2 * EXPERTS), BF16),
        ],
        axis=1,
    )
    home = lax.psum_scatter(packed, "expert", scatter_dimension=0, tiled=True).astype(F32)
    y_two = lax.psum_scatter(
        partial_y.astype(BF16), "expert", scatter_dimension=0, tiled=True
    ).astype(F32)
    total_gate, total_up, total_down = ring_sum(
        jnp.stack(g_gate), jnp.stack(g_up), jnp.stack(g_down)
    )
    outputs = (y_one + y_two).astype(BF16)[None]

    grad_final = cotangent[0].astype(F32)
    grad_weights = home[:, width : width + EXPERTS] + home[:, width + EXPERTS : width + 2 * EXPERTS]
    own = lax.dynamic_slice_in_dim(weights, me * tok_rows, tok_rows, axis=0)
    grad_logits = (
        own * (grad_weights - jnp.sum(own * grad_weights, axis=-1, keepdims=True))
    ).astype(BF16)
    grad_router_w = t_dot(grad_logits, h_two)
    grad_h_two = home[:, :width] + dot_t(grad_logits, w_router)
    grad_gain_two = jnp.sum(grad_h_two * normed_two, axis=0)
    grad_y_one = grad_final + norm_back(grad_h_two * gain_two, normed_two, inv_two)
    grad_attn = grad_y_one.astype(BF16)
    grad_out_w = t_dot(mixed_heads, grad_attn)
    grad_mixed = dot_t(grad_attn, w_out).astype(BF16).reshape(tok_rows, KV, groups, HD)
    grad_probs = jnp.einsum("qkgd,skd->kgqs", grad_mixed, values_all, preferred_element_type=F32)
    grad_values = jnp.einsum(
        "kgqs,qkgd->skd", probs_rounded, grad_mixed, preferred_element_type=F32
    )
    row_dots = jnp.sum(attn_probs * grad_probs, axis=-1, keepdims=True)
    grad_scores = (attn_probs * (grad_probs - row_dots)).astype(BF16)
    grad_keys = (
        jnp.einsum("kgqs,qkgd->skd", grad_scores, queries, preferred_element_type=F32)
        * score_scale
    )
    grad_kv = lax.psum_scatter(
        jnp.concatenate(
            [grad_keys.reshape(seq_rows, KV * HD), grad_values.reshape(seq_rows, KV * HD)], axis=1
        ).astype(BF16),
        "context",
        scatter_dimension=0,
        tiled=True,
    ).astype(F32)
    grad_queries = (
        jnp.einsum("kgqs,skd->qkgd", grad_scores, keys_all, preferred_element_type=F32)
        * score_scale
    )
    grad_q_pre = (
        rotate(grad_queries.reshape(tok_rows, H, HD), cos_table, -sin_table)
        .reshape(tok_rows, H * HD)
        .astype(BF16)
    )
    grad_k_pre = (
        rotate(grad_kv[:, : KV * HD].reshape(tok_rows, KV, HD), cos_table, -sin_table)
        .reshape(tok_rows, KV * HD)
        .astype(BF16)
    )
    grad_v_pre = grad_kv[:, KV * HD :].astype(BF16)
    grad_query_w = t_dot(h_one, grad_q_pre)
    grad_key_w = t_dot(h_one, grad_k_pre)
    grad_value_w = t_dot(h_one, grad_v_pre)
    grad_h_one = (
        dot_t(grad_q_pre, w_query) + dot_t(grad_k_pre, w_key) + dot_t(grad_v_pre, w_value)
    )
    grad_gain_one = jnp.sum(grad_h_one * normed_one, axis=0)
    grad_inputs = grad_y_one + norm_back(grad_h_one * gain_one, normed_one, inv_one)
    grad_tokens = grad_inputs.astype(BF16)[None]
    everywhere = ("expert", "context", "dp")
    small = jnp.concatenate(
        [grad_router_w, grad_gain_one[None], grad_gain_two[None], jnp.zeros((14, width), F32)], axis=0
    )
    total_ors, total_q, total_k, total_v = (
        t.astype(F32)
        for t in lax.psum(
            tuple(
                g.astype(BF16)
                for g in (
                    jnp.concatenate([grad_out_w, small], axis=0),
                    grad_query_w,
                    grad_key_w,
                    grad_value_w,
                )
            ),
            everywhere,
        )
    )
    mid = H * HD
    total_o = total_ors[:mid]
    total_r = total_ors[mid : mid + EXPERTS].T
    total_g1 = total_ors[mid + EXPERTS]
    total_g2 = total_ors[mid + EXPERTS + 1]
    return (
        outputs,
        grad_tokens,
        total_g1,
        total_q,
        total_k,
        total_v,
        total_o,
        total_g2,
        total_r,
        total_gate,
        total_up,
        total_down,
    )


def solution(mesh):
    in_specs = (
        P(("expert", "dp"), "context", None),
        P(),
        P(("expert", "dp"), "context", None),
        P(),
        P(),
        P(),
        P(),
        P(),
        P(),
        P(),
        P("expert", None, None),
        P("expert", None, None),
        P("expert", None, None),
        P(("expert", "dp"), "context", None),
    )
    out_specs = (
        P(("expert", "dp"), "context", None),
        P(("expert", "dp"), "context", None),
        P(),
        P(),
        P(),
        P(),
        P(),
        P(),
        P(),
        P("expert", None, None),
        P("expert", None, None),
        P("expert", None, None),
    )
    return jax.shard_map(body, mesh=mesh, in_specs=in_specs, out_specs=out_specs, check_vma=False)
```

```python
import math

import jax
import jax.numpy as jnp
from jax import lax
from jax.sharding import PartitionSpec as P

H = 16
KV = 8
HD = 64
EXPERTS = 16
SPAN = 128

EPSILON = 1e-06
ROPE_BASE = 10000.0
MASKED = -1e30
F32 = jnp.float32
BF16 = jnp.bfloat16


def rope_tables(positions):
    half_dim = HD // 2
    frequency = ROPE_BASE ** (-(jnp.arange(half_dim, dtype=F32) * 2.0) / HD)
    angles = positions.astype(F32)[:, None] * frequency[None, :]
    return (jnp.cos(angles), jnp.sin(angles))


def rotate(tensor, cos_table, sin_table):
    half_dim = tensor.shape[-1] // 2
    front = tensor[..., :half_dim]
    back = tensor[..., half_dim:]
    cos_wide = cos_table[:, None, :]
    sin_wide = sin_table[:, None, :]
    return jnp.concatenate(
        [front * cos_wide - back * sin_wide, back * cos_wide + front * sin_wide], axis=-1
    )


def positions_of(row_index, span_order):
    block_ids = row_index // SPAN
    picked = jnp.where(
        block_ids[:, None] == jnp.arange(span_order.shape[0], dtype=jnp.int32)[None, :],
        span_order[None, :],
        0,
    )
    return jnp.sum(picked, axis=1, dtype=jnp.int32) * SPAN + row_index % SPAN


def norm_back(grad_normed, normed, inv_root):
    return inv_root * (
        grad_normed - normed * jnp.mean(grad_normed * normed, axis=-1, keepdims=True)
    )


def dot(a, b):
    return jnp.dot(a, b, preferred_element_type=F32)


def dot_t(a, b):
    return lax.dot_general(a, b, (((1,), (1,)), ((), ())), preferred_element_type=F32)


def t_dot(a, b):
    return lax.dot_general(a, b, (((0,), (0,)), ((), ())), preferred_element_type=F32)


def ring_sum(gate, up, down):
    axes = ("context", "dp")
    inner = lax.axis_size("dp")
    size = lax.axis_size("context") * inner
    place = [
        c * inner + (d if c % 2 == 0 else inner - 1 - d)
        for c in range(size // inner)
        for d in range(inner)
    ]
    order = sorted(range(size), key=lambda i: place[i])
    pos = jnp.array(place, jnp.int32)[lax.axis_index(axes)]
    shapes = [a.shape for a in (gate, up, down)]
    gate, up, down = (a.reshape(2, size, -1, a.shape[-1]) for a in (gate, up, down))
    rows, half = gate.shape[2], gate.shape[3]

    def piece(way, index):
        g, u, d = (
            lax.dynamic_index_in_dim(a[way], index, 0, keepdims=False) for a in (gate, up, down)
        )
        return jnp.concatenate([jnp.concatenate([g, u], axis=1), d], axis=0)

    step_of = (1, -1)
    perms = [[(order[i], order[(i + t) % size]) for i in range(size)] for t in step_of]
    held = [piece(way, pos) for way in range(2)]
    for s in range(size - 1):
        for way, t in enumerate(step_of):
            came = lax.ppermute(held[way], axes, perms[way])
            own = piece(way, lax.rem(pos - t * (s + 1) + size, size))
            held[way] = (came.astype(F32) + own.astype(F32)).astype(BF16)
    totals = [jnp.zeros(a.shape, F32) for a in (gate, up, down)]
    for s in range(size):
        for way, t in enumerate(step_of):
            index = lax.rem(pos + t * (1 - s) + size, size)
            now = held[way]
            if s < size - 1:
                held[way] = lax.ppermute(now, axes, perms[way])
            for i, part in enumerate((now[:rows, :half], now[:rows, half:], now[rows:])):
                totals[i] = lax.dynamic_update_slice(
                    totals[i], part.astype(F32)[None, None], (way, index, 0, 0)
                )
    return [a.reshape(shape) for a, shape in zip(totals, shapes)]


def body(
    tokens,
    span_order,
    routes,
    norm_attn,
    w_query,
    w_key,
    w_value,
    w_out,
    norm_moe,
    w_router,
    w_gate,
    w_up,
    w_down,
    cotangent,
):
    tok_rows = tokens.shape[1]
    width = tokens.shape[2]
    seq_rows = tok_rows * lax.axis_size("context")
    groups = H // KV
    score_scale = 1.0 / math.sqrt(HD)
    local_experts = w_gate.shape[0]
    ff = w_gate.shape[2]
    dy_all = lax.all_gather(cotangent[0], "expert", axis=0, tiled=True)
    routes_all = lax.all_gather(routes[0], "expert", axis=0, tiled=True)

    local_index = lax.axis_index("context") * tok_rows + jnp.arange(tok_rows, dtype=jnp.int32)
    pos_query = positions_of(local_index, span_order)
    pos_keys = positions_of(jnp.arange(seq_rows, dtype=jnp.int32), span_order)
    cos_table, sin_table = rope_tables(pos_query)
    allowed = pos_keys[None, :] <= pos_query[:, None]
    inputs = tokens[0].astype(F32)
    inv_one = lax.rsqrt(jnp.mean(inputs * inputs, axis=-1, keepdims=True) + EPSILON)
    normed_one = inputs * inv_one
    gain_one = norm_attn.astype(F32)
    h_one = (normed_one * gain_one).astype(BF16)
    key_pre = dot(h_one, w_key).reshape(tok_rows, KV, HD)
    keys_local = rotate(key_pre, cos_table, sin_table).astype(BF16).reshape(tok_rows, KV * HD)
    values_local = dot(h_one, w_value).astype(BF16)
    kv_all = lax.all_gather(
        jnp.concatenate([keys_local, values_local], axis=1), "context", axis=0, tiled=True
    )
    query_pre = dot(h_one, w_query).reshape(tok_rows, H, HD)
    queries = (
        rotate(query_pre, cos_table, sin_table).astype(BF16).reshape(tok_rows, KV, groups, HD)
    )
    keys_all = kv_all[:, : KV * HD].reshape(seq_rows, KV, HD)
    values_all = kv_all[:, KV * HD :].reshape(seq_rows, KV, HD)
    scores = (
        jnp.einsum("qkgd,skd->kgqs", queries, keys_all, preferred_element_type=F32) * score_scale
    )
    masked = jnp.where(allowed, scores, MASKED)
    top_score = jnp.max(masked, axis=-1, keepdims=True)
    exp_scores = jnp.exp(masked - top_score)
    total_exp = jnp.sum(exp_scores, axis=-1, keepdims=True)
    attn_probs = exp_scores / total_exp
    probs_rounded = attn_probs.astype(BF16)
    mixed_heads = jnp.einsum(
        "kgqs,skd->qkgd", probs_rounded, values_all, preferred_element_type=F32
    )
    mixed_heads = mixed_heads.reshape(tok_rows, H * HD).astype(BF16)
    y_one = inputs + dot(mixed_heads, w_out)
    inv_two = lax.rsqrt(jnp.mean(y_one * y_one, axis=-1, keepdims=True) + EPSILON)
    normed_two = y_one * inv_two
    gain_two = norm_moe.astype(F32)
    h_two = (normed_two * gain_two).astype(BF16)
    h_all = lax.all_gather(h_two, "expert", axis=0, tiled=True)

    experts = jnp.arange(EXPERTS, dtype=jnp.int32)
    chosen = jnp.any(routes_all[:, :, None] == experts[None, None, :], axis=1)
    logits = jnp.where(chosen, dot(h_all, w_router), MASKED)
    weights = jnp.where(chosen, jnp.exp(logits - jnp.max(logits, axis=-1, keepdims=True)), 0.0)
    weights = weights / jnp.sum(weights, axis=-1, keepdims=True)
    me = lax.axis_index("expert")
    mine = lax.dynamic_slice_in_dim(weights, me * local_experts, local_experts, axis=1)

    partial_y = None
    partial_h = None
    dots = []
    g_gate, g_up, g_down = [], [], []
    for e in range(local_experts):
        weight = mine[:, e : e + 1]
        gate_pre = dot(h_all, w_gate[e])
        upward = dot(h_all, w_up[e])
        back = dot_t(dy_all, w_down[e])
        sigmoid_gate = jax.nn.sigmoid(gate_pre)
        silu_gate = gate_pre * sigmoid_gate
        hidden = silu_gate * upward
        hidden_w = (hidden * weight).astype(BF16)
        dots.append(jnp.sum(hidden * back, axis=-1, keepdims=True))
        grad_hidden = back * weight
        grad_gate_pre = (
            grad_hidden * upward * sigmoid_gate * (1.0 + gate_pre * (1.0 - sigmoid_gate))
        ).astype(BF16)
        grad_up_pre = (grad_hidden * silu_gate).astype(BF16)
        add_y = dot(hidden_w, w_down[e])
        add_h = dot_t(grad_gate_pre, w_gate[e]) + dot_t(grad_up_pre, w_up[e])
        partial_y = add_y if partial_y is None else partial_y + add_y
        partial_h = add_h if partial_h is None else partial_h + add_h
        g_down.append(t_dot(hidden_w, dy_all).astype(BF16))
        g_gate.append(t_dot(h_all, grad_gate_pre).astype(BF16))
        g_up.append(t_dot(h_all, grad_up_pre).astype(BF16))

    d_weights = jnp.concatenate(dots, axis=1)
    d_wide = lax.dynamic_update_slice_in_dim(
        jnp.zeros((d_weights.shape[0], EXPERTS), F32), d_weights, me * local_experts, axis=1
    )
    d_high = lax.reduce_precision(d_wide, 8, 7)
    packed = jnp.concatenate(
        [
            partial_h.astype(BF16),
            d_high.astype(BF16),
            (d_wide - d_high).astype(BF16),
            jnp.zeros((d_wide.shape[0], 128 - 2 * EXPERTS), BF16),
        ],
        axis=1,
    )
    home = lax.psum_scatter(packed, "expert", scatter_dimension=0, tiled=True).astype(F32)
    home, later_y = lax.optimization_barrier((home, partial_y.astype(BF16)))
    y_two = lax.psum_scatter(
        later_y, "expert", scatter_dimension=0, tiled=True
    ).astype(F32)
    total_gate, total_up, total_down = ring_sum(
        jnp.stack(g_gate), jnp.stack(g_up), jnp.stack(g_down)
    )
    outputs = (y_one + y_two).astype(BF16)[None]

    grad_final = cotangent[0].astype(F32)
    grad_weights = home[:, width : width + EXPERTS] + home[:, width + EXPERTS : width + 2 * EXPERTS]
    own = lax.dynamic_slice_in_dim(weights, me * tok_rows, tok_rows, axis=0)
    grad_logits = (
        own * (grad_weights - jnp.sum(own * grad_weights, axis=-1, keepdims=True))
    ).astype(BF16)
    grad_router_w = t_dot(grad_logits, h_two)
    grad_h_two = home[:, :width] + dot_t(grad_logits, w_router)
    grad_gain_two = jnp.sum(grad_h_two * normed_two, axis=0)
    grad_y_one = grad_final + norm_back(grad_h_two * gain_two, normed_two, inv_two)
    grad_attn = grad_y_one.astype(BF16)
    grad_out_w = t_dot(mixed_heads, grad_attn)
    grad_mixed = dot_t(grad_attn, w_out).astype(BF16).reshape(tok_rows, KV, groups, HD)
    grad_probs = jnp.einsum("qkgd,skd->kgqs", grad_mixed, values_all, preferred_element_type=F32)
    grad_values = jnp.einsum(
        "kgqs,qkgd->skd", probs_rounded, grad_mixed, preferred_element_type=F32
    )
    row_dots = jnp.sum(attn_probs * grad_probs, axis=-1, keepdims=True)
    grad_scores = (attn_probs * (grad_probs - row_dots)).astype(BF16)
    grad_keys = (
        jnp.einsum("kgqs,qkgd->skd", grad_scores, queries, preferred_element_type=F32)
        * score_scale
    )
    grad_kv = lax.psum_scatter(
        jnp.concatenate(
            [grad_keys.reshape(seq_rows, KV * HD), grad_values.reshape(seq_rows, KV * HD)], axis=1
        ).astype(BF16),
        "context",
        scatter_dimension=0,
        tiled=True,
    ).astype(F32)
    grad_queries = (
        jnp.einsum("kgqs,skd->qkgd", grad_scores, keys_all, preferred_element_type=F32)
        * score_scale
    )
    grad_q_pre = (
        rotate(grad_queries.reshape(tok_rows, H, HD), cos_table, -sin_table)
        .reshape(tok_rows, H * HD)
        .astype(BF16)
    )
    grad_k_pre = (
        rotate(grad_kv[:, : KV * HD].reshape(tok_rows, KV, HD), cos_table, -sin_table)
        .reshape(tok_rows, KV * HD)
        .astype(BF16)
    )
    grad_v_pre = grad_kv[:, KV * HD :].astype(BF16)
    grad_query_w = t_dot(h_one, grad_q_pre)
    grad_key_w = t_dot(h_one, grad_k_pre)
    grad_value_w = t_dot(h_one, grad_v_pre)
    grad_h_one = (
        dot_t(grad_q_pre, w_query) + dot_t(grad_k_pre, w_key) + dot_t(grad_v_pre, w_value)
    )
    grad_gain_one = jnp.sum(grad_h_one * normed_one, axis=0)
    grad_inputs = grad_y_one + norm_back(grad_h_one * gain_one, normed_one, inv_one)
    grad_tokens = grad_inputs.astype(BF16)[None]
    mid, kvw = H * HD, KV * HD
    small = jnp.concatenate([grad_router_w, grad_gain_one[None], grad_gain_two[None]], axis=0)
    small = jnp.pad(small, ((0, 64 - EXPERTS - 2), (0, 2 * mid)))
    packed_grads = jnp.concatenate(
        [
            jnp.concatenate([grad_query_w, grad_key_w, grad_value_w, grad_out_w], axis=1).astype(BF16),
            small.astype(BF16),
        ],
        axis=0,
    )
    share = lax.psum_scatter(packed_grads, "expert", scatter_dimension=0, tiled=True)
    share = lax.psum(share, ("context", "dp"))
    total = lax.all_gather(share, "expert", axis=0, tiled=True)
    total_q = total[:width, :mid].astype(F32)
    total_k = total[:width, mid : mid + kvw].astype(F32)
    total_v = total[:width, mid + kvw : mid + 2 * kvw].astype(F32)
    total_o = total[:width, 2 * mid :].astype(F32)
    total_r = total[width : width + EXPERTS, :width].astype(F32).T
    total_g1 = total[width + EXPERTS, :width].astype(F32)
    total_g2 = total[width + EXPERTS + 1, :width].astype(F32)
    return (
        outputs,
        grad_tokens,
        total_g1,
        total_q,
        total_k,
        total_v,
        total_o,
        total_g2,
        total_r,
        total_gate,
        total_up,
        total_down,
    )


def solution(mesh):
    in_specs = (
        P(("expert", "dp"), "context", None),
        P(),
        P(("expert", "dp"), "context", None),
        P(),
        P(),
        P(),
        P(),
        P(),
        P(),
        P(),
        P("expert", None, None),
        P("expert", None, None),
        P("expert", None, None),
        P(("expert", "dp"), "context", None),
    )
    out_specs = (
        P(("expert", "dp"), "context", None),
        P(("expert", "dp"), "context", None),
        P(),
        P(),
        P(),
        P(),
        P(),
        P(),
        P(),
        P("expert", None, None),
        P("expert", None, None),
        P("expert", None, None),
    )
    return jax.shard_map(body, mesh=mesh, in_specs=in_specs, out_specs=out_specs, check_vma=False)
```
